32 devices in a mesh: seq: 8 (over z, x), ch: 4 (over y, core).
Axes of the slice: x: 2, y: 2, z: 4, core: 2. Of those that a mesh axis runs over, the one named last changes fastest.
Arguments:
- q_in: bfloat16 [4096, 4096], P('seq', 'ch'), may hold values from -6 to 6
- k_in: bfloat16 [4096, 4096], P('seq', 'ch'), may hold values from -6 to 6
- v_in: bfloat16 [4096, 4096], P('seq', 'ch'), may hold values from -6 to 6
- conv_weight: float32 [3, 7, 4096], P(None, None, 'ch'), may hold values from -2 to 2
- mode_residue: float32 [16, 4096], P(None, 'ch'), may hold values from -3 to 3
- decay_rate: float32 [16, 4096], P(None, 'ch'), may hold values from 0.00012207031 to 0.04
- skip_gain: float32 [4096], P('ch'), may hold values from -4 to 4
- tenant_ids: int32 [32], P('seq'), may hold values from 0 to 7
- valid_length: int32 [1], replicated, may hold values from 3840 to 4096
- reft_proj: bfloat16 [8, 4, 4096], P(None, None, 'ch'), may hold values from -0.25 to 0.25
- reft_weight: bfloat16 [8, 4, 4096], P(None, None, 'ch'), may hold values from -0.25 to 0.25
- reft_bias: float32 [8, 4], replicated, may hold values from -8 to 8
Outputs:
- edited: bfloat16 [4096, 4096], P('seq', 'ch')
The draws below stay inside these ranges and needn't reach their ends.
Inputs may be any that keep to these rules, and one draw needn't show every extreme that they name: `tenant_ids`: the tenant of the positions t * 128 to (t + 1) * 128 - 1. Positions from valid_length on are padding.
All inputs are finite; a program needn't handle non-finite values.
Results may differ from the reference program's by a relative error of at most 0.001.
Values may be sent and summed in bfloat16 or wider, within the bound.
A program may use at most 128 MiB of HBM per device.

```python
import math
import jax
import jax.numpy as jnp
from jax import lax

D = 4096
S_DEV = 512
MODES = 16
WIDTH_SHORT = 7
RANK = 4
TENANTS = 8
SPAN = 128
TOKENS = 4096


def place_ends(values, own_key, smallest, high):
    longest = values.shape.index(max(values.shape))
    spots = []
    for shift in (0, 1):
        where = [jax.random.randint(jax.random.fold_in(own_key, axis), (), 0, length) for axis, length in enumerate(values.shape)]
        where[longest] = (where[longest] + shift) % values.shape[longest]
        spots.append(tuple(where))
    return values.at[spots[0]].set(smallest).at[spots[1]].set(high)


def shard_levels(own_key, dims, cuts, smallest, top_value):
    factor_of, own = 1.0, jax.random.fold_in(own_key, 6)
    for axis_at, shards_of in cuts:
        draws = jnp.exp(jax.random.uniform(jax.random.fold_in(own, axis_at), (shards_of,), jnp.float32, smallest / len(cuts), top_value / len(cuts)))
        factor_of = factor_of * jnp.repeat(draws, dims[axis_at] // shards_of).reshape([-1 if axis == axis_at else 1 for axis in range(len(dims))])
    return factor_of


def noise(own_key, dims, deviation, most, cuts=(), kind=jnp.bfloat16):
    result = deviation * jax.random.normal(own_key, dims, jnp.float32)
    if cuts:
        result = result * shard_levels(own_key, dims, cuts, -0.22, 0.18)
    return jnp.clip(result, -most, most).astype(kind)


def setup_inputs(seed: int = 0) -> dict:
    seeds = jax.random.split(jax.random.key(seed), 13)
    q_in = noise(seeds[0], (TOKENS, D), 1.0, 6.0, ((0, 8), (1, 4)))
    k_in = noise(seeds[1], (TOKENS, D), 1.0, 6.0, ((0, 8), (1, 4)))
    v_in = noise(seeds[2], (TOKENS, D), 1.0, 6.0, ((0, 8), (1, 4)))
    conv_weight = noise(seeds[3], (3, WIDTH_SHORT, D), WIDTH_SHORT ** -0.5, 2.0, ((2, 4),), jnp.float32)
    mode_residue = noise(seeds[4], (MODES, D), 0.5, 3.0, ((1, 4),), jnp.float32)
    decay_rate = jnp.clip(jnp.exp(math.log(0.04) - 5.7920375 * jax.random.uniform(seeds[5], (MODES, D), jnp.float32) ** shard_levels(seeds[5], (MODES, D), ((1, 4),), -0.2, 0.2)), 0.00012207031, 0.04)
    skip_gain = noise(seeds[6], (D,), 1.0, 4.0, ((0, 4),), jnp.float32)
    tenant_ids = place_ends(jax.random.randint(seeds[7], (TOKENS // SPAN,), 0, TENANTS), jax.random.fold_in(seeds[7], 1), 0, TENANTS - 1).astype(jnp.int32)
    valid_length = jax.random.randint(seeds[8], (1,), TOKENS - S_DEV // 2, TOKENS + 1).astype(jnp.int32)
    reft_proj = noise(seeds[9], (TENANTS, RANK, D), (D // 8) ** -0.5, 0.25, ((2, 4),))
    reft_weight = noise(seeds[10], (TENANTS, RANK, D), (D // 8) ** -0.5, 0.25, ((2, 4),))
    reft_bias = noise(seeds[11], (TENANTS, RANK), 2.0, 8.0, (), jnp.float32)
    return {"q_in": q_in, "k_in": k_in, "v_in": v_in, "conv_weight": conv_weight, "mode_residue": mode_residue, "decay_rate": decay_rate, "skip_gain": skip_gain, "tenant_ids": tenant_ids, "valid_length": valid_length, "reft_proj": reft_proj, "reft_weight": reft_weight, "reft_bias": reft_bias}


block_width = 128
highest = lax.Precision.HIGHEST

def short_filter(signal, taps_row):
    reach = taps_row.shape[0]
    length = signal.shape[0]
    padded = jnp.pad(signal, ((reach - 1, 0), (0, 0)))
    total = jnp.zeros_like(signal)
    for offset in range(reach):
        start = reach - 1 - offset
        total = total + taps_row[offset][None, :] * padded[start:start + length]
    return total

def long_filter(driven, kernel):
    length = driven.shape[0]
    spectrum = jnp.fft.rfft(driven, n=2 * length, axis=0) * jnp.fft.rfft(kernel, n=2 * length, axis=0)
    return jnp.fft.irfft(spectrum, n=2 * length, axis=0)[:length].astype(driven.dtype)

def reference(q_in, k_in, v_in, conv_weight, mode_residue, decay_rate, skip_gain, tenant_ids, valid_length, reft_proj, reft_weight, reft_bias):
    length, width = q_in.shape
    blocks = width // block_width
    live = (jnp.arange(length, dtype=jnp.int32) < valid_length[0])[:, None]
    times = jnp.arange(length, dtype=jnp.int32).astype(jnp.float32)

    def split(array):
        return array.reshape(array.shape[0], blocks, block_width).transpose(1, 0, 2)

    def one_block(pieces):
        query, keyed, valued, taps_block, residue, rates, gain = pieces
        taps_block = taps_block.reshape(3, -1, block_width)
        query = short_filter(jnp.where(live, query.astype(jnp.float32), 0.0), taps_block[0])
        keyed = short_filter(jnp.where(live, keyed.astype(jnp.float32), 0.0), taps_block[1])
        valued = short_filter(jnp.where(live, valued.astype(jnp.float32), 0.0), taps_block[2])
        driven = keyed * valued
        amplitude = residue * jnp.sqrt(2.0 * rates)
        kernel = lax.optimization_barrier(jnp.sum(jnp.exp(-rates[None] * times[:, None, None]) * amplitude[None], axis=1))
        return query * (long_filter(driven, kernel) + gain[None, :] * driven)
    gated = lax.map(one_block, (split(q_in), split(k_in), split(v_in), split(conv_weight.reshape(-1, width)), split(mode_residue), split(decay_rate), skip_gain.reshape(blocks, block_width)))
    gated = gated.transpose(1, 0, 2).reshape(length, width)
    tenants = reft_bias.shape[0]
    rank = reft_bias.shape[1]
    tenant = jnp.repeat(tenant_ids, length // tenant_ids.shape[0])
    choose = (tenant[:, None] == jnp.arange(tenants, dtype=jnp.int32)[None, :]).astype(jnp.float32)
    both_maps = jnp.concatenate([reft_proj, reft_weight], axis=1).astype(jnp.float32).reshape(tenants * 2 * rank, width)
    every = jnp.dot(gated, both_maps.T, precision=highest).reshape(length, tenants, 2 * rank)
    picked = lax.optimization_barrier(jnp.sum(choose[:, :, None] * every, axis=1))
    bias_rows = jnp.dot(choose, reft_bias, precision=highest)
    delta = picked[:, rank:] + bias_rows - picked[:, :rank]
    spread_delta = (choose[:, :, None] * delta[:, None, :]).reshape(length, tenants * rank)
    edit = jnp.dot(spread_delta, reft_proj.astype(jnp.float32).reshape(tenants * rank, width), precision=highest)
    return jnp.where(live, gated + edit, 0.0).astype(jnp.bfloat16)
```

```python
import functools

import jax
import jax.numpy as jnp
from jax import lax
from jax.experimental import pallas as pl
from jax.experimental.pallas import tpu as pltpu
from jax.sharding import PartitionSpec as P

LANES = 128
UNROLL = 8
PAD = 8
HALO = 16
F32 = jnp.float32
BF16 = jnp.bfloat16


def spread(src, dst, start, limit):
    rows, width = src.shape
    step = min(64, rows)

    def body(block, carry):
        first = pl.multiple_of(block * step, step)
        row = first + lax.broadcasted_iota(jnp.int32, (step, LANES), 0)
        for group in range(width // LANES):
            value = src[pl.ds(first, step), group * LANES : (group + 1) * LANES].astype(F32)
            dst[pl.ds(start + first, step), group, :] = jnp.where(row < limit, value, 0.0)
        return carry

    lax.fori_loop(0, rows // step, body, 0)


def spread_small(src, dst, start):
    rows, width = src.shape
    for group in range(width // LANES):
        dst[start : start + rows, group, :] = src[:, group * LANES : (group + 1) * LANES]


def short_block(ref, taps, base, reach, first):
    window = [ref[first + PAD - reach + 1 + i] for i in range(UNROLL + reach - 1)]
    total = [None] * UNROLL
    for offset in range(reach):
        weight = taps[base + offset]
        for i in range(UNROLL):
            term = weight * window[i + reach - 1 - offset]
            total[i] = term if total[i] is None else total[i] + term
    return total


def scan_kernel(
    valid_ref, q_ref, k_ref, v_ref, halo_ref, taps_ref, residue_ref, rate_ref, gain_ref,
    partial_ref, query_ref, final_ref, q_rows, k_rows, v_rows, taps, decay, scale,
):
    rows, width = q_ref.shape
    reach = taps_ref.shape[1]
    modes = rate_ref.shape[0]
    limit = valid_ref[0] - lax.axis_index("seq") * rows
    for i, (ref, dst) in enumerate(((q_ref, q_rows), (k_ref, k_rows), (v_ref, v_rows))):
        spread(ref, dst, PAD, limit)
        row = lax.broadcasted_iota(jnp.int32, (PAD, LANES), 0) - PAD
        for group in range(width // LANES):
            piece = halo_ref[i, :, group * LANES : (group + 1) * LANES].astype(F32)[HALO - PAD :]
            dst[0:PAD, group, :] = jnp.where(row < limit, piece, 0.0)
        spread_small(taps_ref.at[i], taps, i * reach)
    spread_small(rate_ref, decay, 0)
    spread_small(residue_ref, scale, 0)
    rates = decay[...]
    scale[...] = scale[...] * jnp.sqrt(2.0 * rates)
    decay[...] = jnp.exp(-rates)
    gain = gain_ref[...]

    def body(block, states):
        first = block * UNROLL
        keyed = short_block(k_rows, taps, reach, reach, first)
        valued = short_block(v_rows, taps, 2 * reach, reach, first)
        driven = [a * b for a, b in zip(keyed, valued)]
        query = short_block(q_rows, taps, 0, reach, first)
        for i in range(UNROLL):
            query_ref[first + i] = query[i]
        total = [gain * x for x in driven]
        after = []
        for n in range(modes):
            state, d, a = states[n], decay[n], scale[n]
            for i in range(UNROLL):
                state = d * state + driven[i]
                total[i] = total[i] + a * state
            after.append(state)
        for i in range(UNROLL):
            partial_ref[first + i] = total[i]
        return tuple(after)

    zero = jnp.zeros((width // LANES, LANES), F32)
    states = lax.fori_loop(0, rows // UNROLL, body, (zero,) * modes)
    for n in range(modes):
        final_ref[n] = states[n]


def gate_kernel(
    tenant_ref, partial_ref, query_ref, carry_ref, residue_ref, rate_ref, proj_ref, weight_ref,
    gated_ref, sums_ref, mixed, decay, scale, maps,
):
    rows, width = gated_ref.shape
    modes = rate_ref.shape[0]
    spans = tenant_ref.shape[0]
    span = rows // spans
    rank = proj_ref.shape[1]
    spread_small(rate_ref, decay, 0)
    spread_small(residue_ref, scale, 0)
    rates = decay[...]
    decay[...] = jnp.exp(-rates)
    scale[...] = scale[...] * jnp.sqrt(2.0 * rates) * decay[...] * carry_ref[...]

    def body(block, states):
        first = block * UNROLL
        total = [partial_ref[first + i] for i in range(UNROLL)]
        after = []
        for n in range(modes):
            state, d = states[n], decay[n]
            for i in range(UNROLL):
                total[i] = total[i] + state
                state = state * d
            after.append(state)
        for i in range(UNROLL):
            mixed[first + i] = total[i] * query_ref[first + i]
        return tuple(after)

    lax.fori_loop(0, rows // UNROLL, body, tuple(scale[n] for n in range(modes)))

    def gather(block, carry):
        first = pl.multiple_of(block * 64, 64)
        for group in range(width // LANES):
            gated_ref[pl.ds(first, 64), group * LANES : (group + 1) * LANES] = mixed[
                pl.ds(first, 64), group, :
            ]
        return carry

    lax.fori_loop(0, rows // 64, gather, 0)
    for s in range(spans):
        tenant = tenant_ref[s]
        maps[0:rank, :] = proj_ref[tenant].astype(F32)
        maps[rank : 2 * rank, :] = weight_ref[tenant].astype(F32)
        both = maps[...].astype(BF16)
        value = gated_ref[s * span : (s + 1) * span, :]
        high = value.astype(BF16)
        low = (value - high.astype(F32)).astype(BF16)
        dims = (((1,), (1,)), ((), ()))
        sums_ref[:, s * span : (s + 1) * span] = lax.dot_general(
            both, high, dims, preferred_element_type=F32
        ) + lax.dot_general(both, low, dims, preferred_element_type=F32)


def edit_kernel(tenant_ref, valid_ref, bias_ref, gated_ref, sums_ref, proj_ref, out_ref, maps):
    rows, width = gated_ref.shape
    spans = tenant_ref.shape[0]
    span = rows // spans
    rank = proj_ref.shape[1]
    limit = valid_ref[0] - lax.axis_index("seq") * rows
    line = lax.broadcasted_iota(jnp.int32, (2 * rank, span), 0)
    for s in range(spans):
        tenant = tenant_ref[s]
        maps[0:rank, :] = proj_ref[tenant].astype(F32)
        maps[rank : 2 * rank, :] = proj_ref[tenant].astype(F32)
        totals = sums_ref[:, s * span : (s + 1) * span]
        bias = jnp.zeros((2 * rank, span), F32)
        for r in range(rank):
            bias = jnp.where(line % rank == r, bias_ref[tenant, r], bias)
        change = pltpu.roll(totals, rank, 0) - totals
        delta = jnp.where(line < rank, change, -change) + bias
        high = delta.astype(BF16).astype(F32)
        parts = jnp.where(line < rank, high, delta - high).astype(BF16)
        edit = lax.dot_general(
            parts, maps[...].astype(BF16), (((0,), (0,)), ((), ())), preferred_element_type=F32
        )
        row = s * span + lax.broadcasted_iota(jnp.int32, (span, width), 0)
        value = gated_ref[s * span : (s + 1) * span, :] + edit
        out_ref[s * span : (s + 1) * span, :] = jnp.where(row < limit, value, 0.0).astype(BF16)


def shifted(value, axis, steps):
    count = lax.axis_size(axis)
    return lax.ppermute(value, axis, [(i, i + steps) for i in range(count - steps)])


VMEM = pl.BlockSpec(memory_space=pltpu.VMEM)
SMEM = pl.BlockSpec(memory_space=pltpu.SMEM)


def local(
    q_in, k_in, v_in, conv_weight, mode_residue, decay_rate, skip_gain, tenant_ids, valid_length,
    reft_proj, reft_weight, reft_bias,
):
    rows, width = q_in.shape
    groups = width // LANES
    modes = decay_rate.shape[0]
    reach = conv_weight.shape[1]
    rank = reft_bias.shape[1]
    count = lax.axis_size("seq")
    params = pltpu.CompilerParams(vmem_limit_bytes=48 * 2**20)
    halo = shifted(jnp.stack([x[rows - HALO :] for x in (q_in, k_in, v_in)]), "seq", 1)
    tall = pltpu.VMEM((rows + PAD, groups, LANES), F32)
    small = pltpu.VMEM((modes, groups, LANES), F32)
    cube = jax.ShapeDtypeStruct((rows, groups, LANES), F32)
    partial, query, final = pl.pallas_call(
        scan_kernel,
        out_shape=(cube, cube, jax.ShapeDtypeStruct((modes, groups, LANES), F32)),
        in_specs=[SMEM] + [VMEM] * 8,
        out_specs=(VMEM,) * 3,
        scratch_shapes=[tall, tall, tall, pltpu.VMEM((3 * reach, groups, LANES), F32), small, small],
        compiler_params=params,
    )(
        valid_length, q_in, k_in, v_in, halo, conv_weight, mode_residue, decay_rate,
        skip_gain.reshape(groups, LANES),
    )
    rates = decay_rate.reshape(modes, groups, LANES)
    carry = shifted(final, "seq", 1)
    step = 1
    while step < count:
        carry = carry + jnp.exp(-float(step * rows) * rates) * shifted(carry, "seq", step)
        step *= 2
    gated, sums = pl.pallas_call(
        gate_kernel,
        out_shape=(
            jax.ShapeDtypeStruct((rows, width), F32),
            jax.ShapeDtypeStruct((2 * rank, rows), F32),
        ),
        in_specs=[SMEM] + [VMEM] * 7,
        out_specs=(VMEM,) * 2,
        scratch_shapes=[
            pltpu.VMEM((rows, groups, LANES), F32), small, small, pltpu.VMEM((2 * rank, width), F32),
        ],
        compiler_params=params,
    )(tenant_ids, partial, query, carry, mode_residue, decay_rate, reft_proj, reft_weight)
    totals = lax.psum(sums, "ch")
    return pl.pallas_call(
        edit_kernel,
        out_shape=jax.ShapeDtypeStruct((rows, width), BF16),
        in_specs=[SMEM] * 3 + [VMEM] * 3,
        out_specs=VMEM,
        scratch_shapes=[pltpu.VMEM((2 * rank, width), F32)],
        compiler_params=params,
    )(tenant_ids, valid_length, reft_bias, gated, totals, reft_proj)


def solution(mesh):
    return jax.shard_map(
        local,
        mesh=mesh,
        in_specs=(
            P("seq", "ch"),
            P("seq", "ch"),
            P("seq", "ch"),
            P(None, None, "ch"),
            P(None, "ch"),
            P(None, "ch"),
            P("ch"),
            P("seq"),
            P(),
            P(None, None, "ch"),
            P(None, None, "ch"),
            P(),
        ),
        out_specs=P("seq", "ch"),
        check_vma=False,
    )
```

```python
import functools

import jax
import jax.numpy as jnp
from jax import lax
from jax.experimental import pallas as pl
from jax.experimental.pallas import tpu as pltpu
from jax.sharding import PartitionSpec as P

LANES = 128
UNROLL = 8
PAD = 8
HALO = 16
F32 = jnp.float32
BF16 = jnp.bfloat16


def spread(src, dst, start, limit):
    rows, width = src.shape
    step = min(64, rows)

    def body(block, carry):
        first = pl.multiple_of(block * step, step)
        row = first + lax.broadcasted_iota(jnp.int32, (step, LANES), 0)
        for group in range(width // LANES):
            value = src[pl.ds(first, step), group * LANES : (group + 1) * LANES].astype(F32)
            dst[pl.ds(start + first, step), group, :] = jnp.where(row < limit, value, 0.0)
        return carry

    lax.fori_loop(0, rows // step, body, 0)


def spread_small(src, dst, start):
    rows, width = src.shape
    for group in range(width // LANES):
        dst[start : start + rows, group, :] = src[:, group * LANES : (group + 1) * LANES]


def short_block(ref, taps, base, reach, first):
    window = [ref[first + PAD - reach + 1 + i] for i in range(UNROLL + reach - 1)]
    total = [None] * UNROLL
    for offset in range(reach):
        weight = taps[base + offset]
        for i in range(UNROLL):
            term = weight * window[i + reach - 1 - offset]
            total[i] = term if total[i] is None else total[i] + term
    return total


def kernel(
    early, shifts,
    tenant_ref, valid_ref, bias_ref, q_hbm, k_hbm, v_hbm, taps_hbm, residue_hbm, rate_hbm, gain_hbm,
    proj_hbm, weight_hbm, out_ref,
    q_in, k_in, v_in, taps_in, residue_in, rate_in, gain_in, proj_in, weight_in,
    q_rows, k_rows, v_rows, driven_rows, partial_rows, query_rows, mixed, gated,
    taps, decay, scale, grown, halo, ends, incoming, maps, sums, arrived,
    local_sem, halo_send, halo_recv, state_send, state_recv, sum_send, sum_recv,
):
    rows, width = gated.shape
    groups = width // LANES
    reach = taps_in.shape[1]
    modes = rate_in.shape[0]
    spans = tenant_ref.shape[0]
    span = rows // spans
    rank = proj_in.shape[1]
    blocks = rows // UNROLL
    index, count = lax.axis_index("seq"), lax.axis_size("seq")
    place, places = lax.axis_index("ch"), lax.axis_size("ch")
    limit = valid_ref[0] - index * rows

    def remote(src, dst, send, recv, seq, ch):
        return pltpu.make_async_remote_copy(
            src_ref=src, dst_ref=dst, send_sem=send, recv_sem=recv,
            device_id=(seq, ch), device_id_type=pl.DeviceIdType.MESH,
        )

    barrier = pltpu.get_barrier_semaphore()
    steps = sorted({step for group in shifts for step in group})

    def greet(seq, ch):
        pl.semaphore_signal(
            barrier, inc=1, device_id=(seq, ch), device_id_type=pl.DeviceIdType.MESH
        )

    for step in steps:
        pl.when(index + step < count)(lambda step=step: greet(index + step, place))
        pl.when(index >= step)(lambda step=step: greet(index - step, place))
    for offset in range(1, places):
        greet(index, lax.rem(place + offset, places))

    pairs = (
        (k_hbm, k_in), (v_hbm, v_in), (taps_hbm, taps_in), (residue_hbm, residue_in),
        (rate_hbm, rate_in), (gain_hbm, gain_in), (q_hbm, q_in), (proj_hbm, proj_in),
        (weight_hbm, weight_in),
    )
    loads = [
        pltpu.make_async_copy(src, dst, local_sem.at[i]) for i, (src, dst) in enumerate(pairs)
    ]
    for load in loads:
        load.start()
    loads[0].wait()
    spread(k_in, k_rows, PAD, limit)

    peers = places - 1
    for step in steps:
        peers = peers + (index + step < count).astype(jnp.int32)
        peers = peers + (index >= step).astype(jnp.int32)
    pl.semaphore_wait(barrier, peers)

    halos = [
        remote(
            src.at[pl.ds(rows - HALO, HALO)], halo.at[i], halo_send.at[i], halo_recv.at[i],
            index + 1, place,
        )
        for i, src in enumerate((q_hbm, k_hbm, v_hbm))
    ]

    @pl.when(index + 1 < count)
    def _():
        for copy in halos:
            copy.start()

    loads[1].wait()
    spread(v_in, v_rows, PAD, limit)
    for load in loads[2:6]:
        load.wait()
    for i in range(3):
        spread_small(taps_in.at[i], taps, i * reach)
    spread_small(rate_in, grown, 0)
    spread_small(residue_in, scale, 0)
    scale[...] = scale[...] * jnp.sqrt(2.0 * grown[...])
    decay[...] = jnp.exp(-grown[...])

    def drive(first, states):
        keyed = short_block(k_rows, taps, reach, reach, first)
        valued = short_block(v_rows, taps, 2 * reach, reach, first)
        driven = [x * y for x, y in zip(keyed, valued)]
        for i in range(UNROLL):
            driven_rows[first + i] = driven[i]
        after = []
        for n in range(modes):
            d, state = decay[n], states[n]
            for i in range(UNROLL):
                state = driven[i] if state is None else d * state + driven[i]
            after.append(state)
        return tuple(after)

    zeros = (jnp.zeros((groups, LANES), F32),) * modes
    states = lax.fori_loop(1, blocks, lambda b, c: drive(b * UNROLL, c), zeros)
    for n in range(modes):
        ends[0, n] = states[n]

    pl.when(index >= 1)(lambda: [copy.wait_recv() for copy in halos] and None)

    @pl.when(index == 0)
    def _():
        halo[...] = jnp.zeros_like(halo)

    for i, dst in enumerate((q_rows, k_rows, v_rows)):
        row = lax.broadcasted_iota(jnp.int32, (PAD, LANES), 0) - PAD
        for group in range(groups):
            piece = halo[i, :, group * LANES : (group + 1) * LANES].astype(F32)[HALO - PAD :]
            dst[0:PAD, group, :] = jnp.where(row < limit, piece, 0.0)
    states = drive(0, (None,) * modes)
    for n in range(modes):
        ends[0, n] = ends[0, n] + jnp.exp(-float(rows - UNROLL) * grown[n]) * states[n]

    slot = 0
    rounds = []
    for stage, group in enumerate(shifts):
        copies = []
        for step in group:
            copies.append((step, slot, remote(
                ends.at[stage], incoming.at[slot], state_send.at[slot], state_recv.at[slot],
                index + step, place,
            )))
            slot += 1
        rounds.append(copies)

    def send(stage):
        for step, _, copy in rounds[stage]:
            pl.when(index + step < count)(copy.start)

    send(0)
    loads[6].wait()
    spread(q_in, q_rows, PAD, limit)
    gain = gain_in[...]

    def scan(gate, block, states):
        first = block * UNROLL
        driven = [driven_rows[first + i] for i in range(UNROLL)]
        total = [gain * x for x in driven]
        after = []
        for n in range(modes):
            state, d, a = states[n], decay[n], scale[n]
            for i in range(UNROLL):
                state = d * state + driven[i]
                total[i] = total[i] + a * state
            after.append(state)
        query = short_block(q_rows, taps, 0, reach, first)
        for i in range(UNROLL):
            if gate:
                mixed[first + i] = query[i] * total[i]
            else:
                partial_rows[first + i] = total[i]
                query_rows[first + i] = query[i]
        return tuple(after)

    cut = early * span // UNROLL
    states = zeros
    done = 0
    for stage, copies in enumerate(rounds):
        stop = cut * (stage + 1) // len(rounds)
        states = lax.fori_loop(done, stop, functools.partial(scan, False), states)
        done = stop
        first_round = stage == 0
        if first_round:
            ends[1] = jnp.zeros((modes, groups, LANES), F32)
        else:
            ends[stage + 1] = ends[stage]
        covered = 0 if first_round else copies[0][0]
        for step, where, copy in copies:
            factor = float((step - 1 if first_round else covered) * rows)

            @pl.when(index >= step)
            def _():
                copy.wait_recv()
                ends[stage + 1] = ends[stage + 1] + jnp.exp(-factor * grown[...]) * incoming[where]

        if stage + 1 < len(rounds):
            send(stage + 1)

    last = len(rounds)
    if cut < blocks:
        states = tuple(
            states[n] + jnp.exp(-float(cut * UNROLL) * grown[n]) * ends[last, n]
            for n in range(modes)
        )

    def correct(block, states):
        first = block * UNROLL
        total = [partial_rows[first + i] for i in range(UNROLL)]
        after = []
        for n in range(modes):
            state, d = states[n], decay[n]
            for i in range(UNROLL):
                total[i] = total[i] + state
                state = state * d
            after.append(state)
        for i in range(UNROLL):
            mixed[first + i] = total[i] * query_rows[first + i]
        return tuple(after)

    def gather(block, carry):
        first = pl.multiple_of(block * 64, 64)
        for group in range(groups):
            gated[pl.ds(first, 64), group * LANES : (group + 1) * LANES] = mixed[
                pl.ds(first, 64), group, :
            ]
        return carry

    loads[7].wait()
    loads[8].wait()
    order = list(range(early, spans)) + list(range(early))
    sends = {}
    per = span // UNROLL
    for s in order:
        if s == 0:
            states = tuple(scale[n] * decay[n] * ends[last, n] for n in range(modes))
        body = functools.partial(scan, True) if s >= early else correct
        states = lax.fori_loop(s * per, (s + 1) * per, body, states)
        lax.fori_loop(s * span // 64, (s + 1) * span // 64, gather, 0)
        tenant = tenant_ref[s]
        maps[0:rank, :] = proj_in[tenant].astype(F32)
        maps[rank : 2 * rank, :] = weight_in[tenant].astype(F32)
        both = maps[...].astype(BF16)
        value = gated[s * span : (s + 1) * span, :]
        high = value.astype(BF16)
        low = (value - high.astype(F32)).astype(BF16)
        dims = (((1,), (1,)), ((), ()))
        sums[s] = lax.dot_general(
            both, high, dims, preferred_element_type=F32
        ) + lax.dot_general(both, low, dims, preferred_element_type=F32)
        sends[s] = [
            remote(
                sums.at[s], arrived.at[offset - 1, s], sum_send.at[offset - 1, s],
                sum_recv.at[offset - 1, s], index, lax.rem(place + offset, places),
            )
            for offset in range(1, places)
        ]
        for copy in sends[s]:
            copy.start()

    line = lax.broadcasted_iota(jnp.int32, (2 * rank, span), 0)
    for s in order:
        tenant = tenant_ref[s]
        maps[0:rank, :] = proj_in[tenant].astype(F32)
        maps[rank : 2 * rank, :] = proj_in[tenant].astype(F32)
        totals = sums[s]
        for offset in range(1, places):
            sends[s][offset - 1].wait_recv()
            totals = totals + arrived[offset - 1, s]
        bias = jnp.zeros((2 * rank, span), F32)
        for r in range(rank):
            bias = jnp.where(line % rank == r, bias_ref[tenant, r], bias)
        change = pltpu.roll(totals, rank, 0) - totals
        delta = jnp.where(line < rank, change, -change) + bias
        high = delta.astype(BF16).astype(F32)
        parts = jnp.where(line < rank, high, delta - high).astype(BF16)
        edit = lax.dot_general(
            parts, maps[...].astype(BF16), (((0,), (0,)), ((), ())), preferred_element_type=F32
        )
        row = s * span + lax.broadcasted_iota(jnp.int32, (span, width), 0)
        value = gated[s * span : (s + 1) * span, :] + edit
        out_ref[s * span : (s + 1) * span, :] = jnp.where(row < limit, value, 0.0).astype(BF16)

    @pl.when(index + 1 < count)
    def _():
        for copy in halos:
            copy.wait_send()

    for copies in rounds:
        for step, _, copy in copies:
            pl.when(index + step < count)(copy.wait_send)
    for s in order:
        for copy in sends[s]:
            copy.wait_send()


VMEM = pl.BlockSpec(memory_space=pltpu.VMEM)
SMEM = pl.BlockSpec(memory_space=pltpu.SMEM)
HBM = pl.BlockSpec(memory_space=pl.ANY)


def local(
    q_in, k_in, v_in, conv_weight, mode_residue, decay_rate, skip_gain, tenant_ids, valid_length,
    reft_proj, reft_weight, reft_bias,
):
    rows, width = q_in.shape
    groups = width // LANES
    modes = decay_rate.shape[0]
    reach = conv_weight.shape[1]
    rank = reft_bias.shape[1]
    spans = tenant_ids.shape[0]
    count, places = lax.axis_size("seq"), lax.axis_size("ch")
    shifts = [(1, 2)]
    while 2 ** len(shifts) < count:
        shifts.append((2 ** len(shifts),))
    slots = len(shifts) + 1
    gain = skip_gain.reshape(groups, LANES)
    args = (q_in, k_in, v_in, conv_weight, mode_residue, decay_rate, gain, reft_proj, reft_weight)
    tall = pltpu.VMEM((rows + PAD, groups, LANES), F32)
    cube = pltpu.VMEM((rows, groups, LANES), F32)
    small = pltpu.VMEM((modes, groups, LANES), F32)
    dma = pltpu.SemaphoreType.DMA
    return pl.pallas_call(
        functools.partial(kernel, spans - 1, tuple(shifts)),
        out_shape=jax.ShapeDtypeStruct((rows, width), BF16),
        in_specs=[SMEM] * 3 + [HBM] * 9,
        out_specs=VMEM,
        scratch_shapes=[pltpu.VMEM(x.shape, x.dtype) for x in args]
        + [tall, tall, tall, cube, cube, cube, cube, pltpu.VMEM((rows, width), F32)]
        + [pltpu.VMEM((3 * reach, groups, LANES), F32), small, small, small]
        + [
            pltpu.VMEM((3, HALO, width), BF16),
            pltpu.VMEM((slots, modes, groups, LANES), F32),
            pltpu.VMEM((slots, modes, groups, LANES), F32),
            pltpu.VMEM((2 * rank, width), F32),
            pltpu.VMEM((spans, 2 * rank, rows // spans), F32),
            pltpu.VMEM((places - 1, spans, 2 * rank, rows // spans), F32),
        ]
        + [dma((len(args),)), dma((3,)), dma((3,)), dma((slots,)), dma((slots,))]
        + [dma((places - 1, spans)), dma((places - 1, spans))],
        compiler_params=pltpu.CompilerParams(
            collective_id=0, has_side_effects=True, vmem_limit_bytes=56 * 2**20
        ),
    )(tenant_ids, valid_length, reft_bias, *args)


def solution(mesh):
    return jax.shard_map(
        local,
        mesh=mesh,
        in_specs=(
            P("seq", "ch"),
            P("seq", "ch"),
            P("seq", "ch"),
            P(None, None, "ch"),
            P(None, "ch"),
            P(None, "ch"),
            P("ch"),
            P("seq"),
            P(),
            P(None, None, "ch"),
            P(None, None, "ch"),
            P(),
        ),
        out_specs=P("seq", "ch"),
        check_vma=False,
    )
```

```python
import functools

import jax
import jax.numpy as jnp
from jax import lax
from jax.experimental import pallas as pl
from jax.experimental.pallas import tpu as pltpu
from jax.sharding import PartitionSpec as P

LANES = 128
UNROLL = 8
PAD = 8
HALO = 16
F32 = jnp.float32
BF16 = jnp.bfloat16


def spread(src, dst, start, limit):
    rows, width = src.shape
    step = min(64, rows)

    def body(block, carry):
        first = pl.multiple_of(block * step, step)
        row = first + lax.broadcasted_iota(jnp.int32, (step, LANES), 0)
        for group in range(width // LANES):
            value = src[pl.ds(first, step), group * LANES : (group + 1) * LANES].astype(F32)
            dst[pl.ds(start + first, step), group, :] = jnp.where(row < limit, value, 0.0)
        return carry

    lax.fori_loop(0, rows // step, body, 0)


def spread_small(src, dst, start):
    rows, width = src.shape
    for group in range(width // LANES):
        dst[start : start + rows, group, :] = src[:, group * LANES : (group + 1) * LANES]


def short_block(ref, taps, base, reach, first):
    window = [ref[first + PAD - reach + 1 + i] for i in range(UNROLL + reach - 1)]
    total = [None] * UNROLL
    for offset in range(reach):
        weight = taps[base + offset]
        for i in range(UNROLL):
            term = weight * window[i + reach - 1 - offset]
            total[i] = term if total[i] is None else total[i] + term
    return total


def kernel(
    early, shifts,
    tenant_ref, valid_ref, bias_ref, q_hbm, k_hbm, v_hbm, taps_hbm, residue_hbm, rate_hbm, gain_hbm,
    proj_hbm, weight_hbm, out_hbm,
    q_in, k_in, v_in, taps_in, residue_in, rate_in, gain_in, proj_in, weight_in,
    q_rows, k_rows, v_rows, driven_rows, partial_rows, query_rows, mixed, gated,
    taps, decay, scale, grown, halo, ends, incoming, maps, sums, arrived,
    local_sem, halo_send, halo_recv, state_send, state_recv, sum_send, sum_recv, out_ref, out_sem,
):
    rows, width = gated.shape
    groups = width // LANES
    reach = taps_in.shape[1]
    modes = rate_in.shape[0]
    spans = tenant_ref.shape[0]
    span = rows // spans
    rank = proj_in.shape[1]
    blocks = rows // UNROLL
    index, count = lax.axis_index("seq"), lax.axis_size("seq")
    place, places = lax.axis_index("ch"), lax.axis_size("ch")
    limit = valid_ref[0] - index * rows

    def remote(src, dst, send, recv, seq, ch):
        return pltpu.make_async_remote_copy(
            src_ref=src, dst_ref=dst, send_sem=send, recv_sem=recv,
            device_id=(seq, ch), device_id_type=pl.DeviceIdType.MESH,
        )

    barrier = pltpu.get_barrier_semaphore()
    steps = sorted({step for group in shifts for step in group})

    def greet(seq, ch):
        pl.semaphore_signal(
            barrier, inc=1, device_id=(seq, ch), device_id_type=pl.DeviceIdType.MESH
        )

    for step in steps:
        pl.when(index + step < count)(lambda step=step: greet(index + step, place))
        pl.when(index >= step)(lambda step=step: greet(index - step, place))
    for offset in range(1, places):
        greet(index, lax.rem(place + offset, places))

    pairs = (
        (k_hbm, k_in), (v_hbm, v_in), (taps_hbm, taps_in), (residue_hbm, residue_in),
        (rate_hbm, rate_in), (gain_hbm, gain_in), (q_hbm, q_in), (proj_hbm, proj_in),
        (weight_hbm, weight_in),
    )
    loads = [
        pltpu.make_async_copy(src, dst, local_sem.at[i]) for i, (src, dst) in enumerate(pairs)
    ]
    for load in loads:
        load.start()
    loads[0].wait()
    spread(k_in, k_rows, PAD, limit)

    peers = places - 1
    for step in steps:
        peers = peers + (index + step < count).astype(jnp.int32)
        peers = peers + (index >= step).astype(jnp.int32)
    pl.semaphore_wait(barrier, peers)

    halos = [
        remote(
            src.at[pl.ds(rows - HALO, HALO)], halo.at[i], halo_send.at[i], halo_recv.at[i],
            index + 1, place,
        )
        for i, src in enumerate((q_hbm, k_hbm, v_hbm))
    ]

    @pl.when(index + 1 < count)
    def _():
        for copy in halos:
            copy.start()

    loads[1].wait()
    spread(v_in, v_rows, PAD, limit)
    for load in loads[2:6]:
        load.wait()
    for i in range(3):
        spread_small(taps_in.at[i], taps, i * reach)
    spread_small(rate_in, grown, 0)
    spread_small(residue_in, scale, 0)
    scale[...] = scale[...] * jnp.sqrt(2.0 * grown[...])
    decay[...] = jnp.exp(-grown[...])

    def drive(first, states):
        keyed = short_block(k_rows, taps, reach, reach, first)
        valued = short_block(v_rows, taps, 2 * reach, reach, first)
        driven = [x * y for x, y in zip(keyed, valued)]
        for i in range(UNROLL):
            driven_rows[first + i] = driven[i]
        after = []
        for n in range(modes):
            d, state = decay[n], states[n]
            for i in range(UNROLL):
                state = driven[i] if state is None else d * state + driven[i]
            after.append(state)
        return tuple(after)

    zeros = (jnp.zeros((groups, LANES), F32),) * modes
    states = lax.fori_loop(1, blocks, lambda b, c: drive(b * UNROLL, c), zeros)
    for n in range(modes):
        ends[0, n] = states[n]

    pl.when(index >= 1)(lambda: [copy.wait_recv() for copy in halos] and None)

    @pl.when(index == 0)
    def _():
        halo[...] = jnp.zeros_like(halo)

    for i, dst in enumerate((q_rows, k_rows, v_rows)):
        row = lax.broadcasted_iota(jnp.int32, (PAD, LANES), 0) - PAD
        for group in range(groups):
            piece = halo[i, :, group * LANES : (group + 1) * LANES].astype(F32)[HALO - PAD :]
            dst[0:PAD, group, :] = jnp.where(row < limit, piece, 0.0)
    states = drive(0, (None,) * modes)
    for n in range(modes):
        ends[0, n] = ends[0, n] + jnp.exp(-float(rows - UNROLL) * grown[n]) * states[n]

    slot = 0
    rounds = []
    for stage, group in enumerate(shifts):
        copies = []
        for step in group:
            copies.append((step, slot, remote(
                ends.at[stage], incoming.at[slot], state_send.at[slot], state_recv.at[slot],
                index + step, place,
            )))
            slot += 1
        rounds.append(copies)

    def send(stage):
        for step, _, copy in rounds[stage]:
            pl.when(index + step < count)(copy.start)

    send(0)
    loads[6].wait()
    spread(q_in, q_rows, PAD, limit)
    gain = gain_in[...]

    def scan(gate, block, states):
        first = block * UNROLL
        driven = [driven_rows[first + i] for i in range(UNROLL)]
        total = [gain * x for x in driven]
        after = []
        for n in range(modes):
            state, d, a = states[n], decay[n], scale[n]
            for i in range(UNROLL):
                state = d * state + driven[i]
                total[i] = total[i] + a * state
            after.append(state)
        query = short_block(q_rows, taps, 0, reach, first)
        for i in range(UNROLL):
            if gate:
                mixed[first + i] = query[i] * total[i]
            else:
                partial_rows[first + i] = total[i]
                query_rows[first + i] = query[i]
        return tuple(after)

    cut = early * span // UNROLL
    states = zeros
    done = 0
    for stage, copies in enumerate(rounds):
        stop = cut * (stage + 1) // len(rounds)
        states = lax.fori_loop(done, stop, functools.partial(scan, False), states)
        done = stop
        first_round = stage == 0
        if first_round:
            ends[1] = jnp.zeros((modes, groups, LANES), F32)
        else:
            ends[stage + 1] = ends[stage]
        covered = 0 if first_round else copies[0][0]
        for step, where, copy in copies:
            factor = float((step - 1 if first_round else covered) * rows)

            @pl.when(index >= step)
            def _():
                copy.wait_recv()
                ends[stage + 1] = ends[stage + 1] + jnp.exp(-factor * grown[...]) * incoming[where]

        if stage + 1 < len(rounds):
            send(stage + 1)

    last = len(rounds)
    if cut < blocks:
        states = tuple(
            states[n] + jnp.exp(-float(cut * UNROLL) * grown[n]) * ends[last, n]
            for n in range(modes)
        )

    def correct(block, states):
        first = block * UNROLL
        total = [partial_rows[first + i] for i in range(UNROLL)]
        after = []
        for n in range(modes):
            state, d = states[n], decay[n]
            for i in range(UNROLL):
                total[i] = total[i] + state
                state = state * d
            after.append(state)
        for i in range(UNROLL):
            mixed[first + i] = total[i] * query_rows[first + i]
        return tuple(after)

    def gather(block, carry):
        first = pl.multiple_of(block * 64, 64)
        for group in range(groups):
            gated[pl.ds(first, 64), group * LANES : (group + 1) * LANES] = mixed[
                pl.ds(first, 64), group, :
            ]
        return carry

    loads[7].wait()
    loads[8].wait()
    order = list(range(early, spans)) + list(range(early))
    sends = {}
    per = span // UNROLL
    for s in order:
        if s == 0:
            states = tuple(scale[n] * decay[n] * ends[last, n] for n in range(modes))
        body = functools.partial(scan, True) if s >= early else correct
        states = lax.fori_loop(s * per, (s + 1) * per, body, states)
        lax.fori_loop(s * span // 64, (s + 1) * span // 64, gather, 0)
        tenant = tenant_ref[s]
        maps[0:rank, :] = proj_in[tenant].astype(F32)
        maps[rank : 2 * rank, :] = weight_in[tenant].astype(F32)
        both = maps[...].astype(BF16)
        value = gated[s * span : (s + 1) * span, :]
        high = value.astype(BF16)
        low = (value - high.astype(F32)).astype(BF16)
        dims = (((1,), (1,)), ((), ()))
        sums[s] = lax.dot_general(
            both, high, dims, preferred_element_type=F32
        ) + lax.dot_general(both, low, dims, preferred_element_type=F32)
        sends[s] = [
            remote(
                sums.at[s], arrived.at[offset - 1, s], sum_send.at[offset - 1, s],
                sum_recv.at[offset - 1, s], index, lax.rem(place + offset, places),
            )
            for offset in range(1, places)
        ]
        for copy in sends[s]:
            copy.start()

    line = lax.broadcasted_iota(jnp.int32, (2 * rank, span), 0)
    stores = []
    for s in order:
        tenant = tenant_ref[s]
        maps[0:rank, :] = proj_in[tenant].astype(F32)
        maps[rank : 2 * rank, :] = proj_in[tenant].astype(F32)
        totals = sums[s]
        for offset in range(1, places):
            sends[s][offset - 1].wait_recv()
            totals = totals + arrived[offset - 1, s]
        bias = jnp.zeros((2 * rank, span), F32)
        for r in range(rank):
            bias = jnp.where(line % rank == r, bias_ref[r, tenant], bias)
        change = pltpu.roll(totals, rank, 0) - totals
        delta = jnp.where(line < rank, change, -change) + bias
        high = delta.astype(BF16).astype(F32)
        parts = jnp.where(line < rank, high, delta - high).astype(BF16)
        edit = lax.dot_general(
            parts, maps[...].astype(BF16), (((0,), (0,)), ((), ())), preferred_element_type=F32
        )
        row = s * span + lax.broadcasted_iota(jnp.int32, (span, width), 0)
        value = gated[s * span : (s + 1) * span, :] + edit
        out_ref[s * span : (s + 1) * span, :] = jnp.where(row < limit, value, 0.0).astype(BF16)
        part = pl.ds(s * span, span)
        stores.append(pltpu.make_async_copy(out_ref.at[part], out_hbm.at[part], out_sem.at[s]))
        stores[-1].start()

    @pl.when(index + 1 < count)
    def _():
        for copy in halos:
            copy.wait_send()

    for copies in rounds:
        for step, _, copy in copies:
            pl.when(index + step < count)(copy.wait_send)
    for s in order:
        for copy in sends[s]:
            copy.wait_send()
    for store in stores:
        store.wait()


VMEM = pl.BlockSpec(memory_space=pltpu.VMEM)
SMEM = pl.BlockSpec(memory_space=pltpu.SMEM)
HBM = pl.BlockSpec(memory_space=pltpu.HBM)


def local(
    q_in, k_in, v_in, conv_weight, mode_residue, decay_rate, skip_gain, tenant_ids, valid_length,
    reft_proj, reft_weight, reft_bias,
):
    rows, width = q_in.shape
    groups = width // LANES
    modes = decay_rate.shape[0]
    reach = conv_weight.shape[1]
    rank = reft_bias.shape[1]
    spans = tenant_ids.shape[0]
    count, places = lax.axis_size("seq"), lax.axis_size("ch")
    shifts = [(1, 2)]
    while 2 ** len(shifts) < count:
        shifts.append((2 ** len(shifts),))
    slots = len(shifts) + 1
    gain = skip_gain.reshape(groups, LANES)
    args = (q_in, k_in, v_in, conv_weight, mode_residue, decay_rate, gain, reft_proj, reft_weight)
    tall = pltpu.VMEM((rows + PAD, groups, LANES), F32)
    cube = pltpu.VMEM((rows, groups, LANES), F32)
    small = pltpu.VMEM((modes, groups, LANES), F32)
    dma = pltpu.SemaphoreType.DMA
    return pl.pallas_call(
        functools.partial(kernel, spans - 1, tuple(shifts)),
        out_shape=jax.ShapeDtypeStruct((rows, width), BF16),
        in_specs=[SMEM] * 3 + [HBM] * 9,
        out_specs=HBM,
        scratch_shapes=[pltpu.VMEM(x.shape, x.dtype) for x in args]
        + [tall, tall, tall, cube, cube, cube, cube, pltpu.VMEM((rows, width), F32)]
        + [pltpu.VMEM((3 * reach, groups, LANES), F32), small, small, small]
        + [
            pltpu.VMEM((3, HALO, width), BF16),
            pltpu.VMEM((slots, modes, groups, LANES), F32),
            pltpu.VMEM((slots, modes, groups, LANES), F32),
            pltpu.VMEM((2 * rank, width), F32),
            pltpu.VMEM((spans, 2 * rank, rows // spans), F32),
            pltpu.VMEM((places - 1, spans, 2 * rank, rows // spans), F32),
        ]
        + [dma((len(args),)), dma((3,)), dma((3,)), dma((slots,)), dma((slots,))]
        + [dma((places - 1, spans)), dma((places - 1, spans))]
        + [pltpu.VMEM((rows, width), BF16), dma((spans,))],
        compiler_params=pltpu.CompilerParams(
            collective_id=0, has_side_effects=True, vmem_limit_bytes=60 * 2**20
        ),
    )(tenant_ids, valid_length, reft_bias.T, *args)


def solution(mesh):
    return jax.shard_map(
        local,
        mesh=mesh,
        in_specs=(
            P("seq", "ch"),
            P("seq", "ch"),
            P("seq", "ch"),
            P(None, None, "ch"),
            P(None, "ch"),
            P(None, "ch"),
            P("ch"),
            P("seq"),
            P(),
            P(None, None, "ch"),
            P(None, None, "ch"),
            P(),
        ),
        out_specs=P("seq", "ch"),
        check_vma=False,
    )
```

```python
import functools

import jax
import jax.numpy as jnp
from jax import lax
from jax.experimental import pallas as pl
from jax.experimental.pallas import tpu as pltpu
from jax.sharding import PartitionSpec as P

LANES = 128
UNROLL = 16
PAD = 8
HALO = 16
F32 = jnp.float32
BF16 = jnp.bfloat16


def spread(src, dst, start, limit):
    rows, width = src.shape
    step = min(64, rows)

    def body(block, carry):
        first = pl.multiple_of(block * step, step)
        row = first + lax.broadcasted_iota(jnp.int32, (step, LANES), 0)
        for group in range(width // LANES):
            value = src[pl.ds(first, step), group * LANES : (group + 1) * LANES].astype(F32)
            dst[pl.ds(start + first, step), group, :] = jnp.where(row < limit, value, 0.0)
        return carry

    lax.fori_loop(0, rows // step, body, 0)


def spread_small(src, dst, start):
    rows, width = src.shape
    for group in range(width // LANES):
        dst[start : start + rows, group, :] = src[:, group * LANES : (group + 1) * LANES]


def short_block(ref, taps, base, reach, first):
    window = [ref[first + PAD - reach + 1 + i] for i in range(UNROLL + reach - 1)]
    total = [None] * UNROLL
    for offset in range(reach):
        weight = taps[base + offset]
        for i in range(UNROLL):
            term = weight * window[i + reach - 1 - offset]
            total[i] = term if total[i] is None else total[i] + term
    return total


def kernel(
    early, shifts,
    tenant_ref, valid_ref, bias_ref, q_hbm, k_hbm, v_hbm, taps_hbm, residue_hbm, rate_hbm, gain_hbm,
    proj_hbm, weight_hbm, out_hbm,
    q_in, k_in, v_in, taps_in, residue_in, rate_in, gain_in, proj_in, weight_in,
    q_rows, k_rows, v_rows, driven_rows, partial_rows, query_rows, mixed, gated,
    taps, decay, scale, grown, halo, ends, incoming, maps, sums, arrived,
    local_sem, halo_send, halo_recv, state_send, state_recv, sum_send, sum_recv, out_ref, out_sem,
):
    rows, width = gated.shape
    groups = width // LANES
    reach = taps_in.shape[1]
    modes = rate_in.shape[0]
    spans = tenant_ref.shape[0]
    span = rows // spans
    rank = proj_in.shape[1]
    blocks = rows // UNROLL
    index, count = lax.axis_index("seq"), lax.axis_size("seq")
    place, places = lax.axis_index("ch"), lax.axis_size("ch")
    limit = valid_ref[0] - index * rows

    def remote(src, dst, send, recv, seq, ch):
        return pltpu.make_async_remote_copy(
            src_ref=src, dst_ref=dst, send_sem=send, recv_sem=recv,
            device_id=(seq, ch), device_id_type=pl.DeviceIdType.MESH,
        )

    barrier = pltpu.get_barrier_semaphore()
    steps = sorted({step for group in shifts for step in group})

    def greet(seq, ch):
        pl.semaphore_signal(
            barrier, inc=1, device_id=(seq, ch), device_id_type=pl.DeviceIdType.MESH
        )

    for step in steps:
        pl.when(index + step < count)(lambda step=step: greet(index + step, place))
        pl.when(index >= step)(lambda step=step: greet(index - step, place))
    for offset in range(1, places):
        greet(index, lax.rem(place + offset, places))

    pairs = (
        (k_hbm, k_in), (v_hbm, v_in), (taps_hbm, taps_in), (residue_hbm, residue_in),
        (rate_hbm, rate_in), (gain_hbm, gain_in), (q_hbm, q_in), (proj_hbm, proj_in),
        (weight_hbm, weight_in),
    )
    loads = [
        pltpu.make_async_copy(src, dst, local_sem.at[i]) for i, (src, dst) in enumerate(pairs)
    ]
    for load in loads:
        load.start()
    loads[0].wait()
    spread(k_in, k_rows, PAD, limit)

    peers = places - 1
    for step in steps:
        peers = peers + (index + step < count).astype(jnp.int32)
        peers = peers + (index >= step).astype(jnp.int32)
    pl.semaphore_wait(barrier, peers)

    halos = [
        remote(
            src.at[pl.ds(rows - HALO, HALO)], halo.at[i], halo_send.at[i], halo_recv.at[i],
            index + 1, place,
        )
        for i, src in enumerate((q_hbm, k_hbm, v_hbm))
    ]

    @pl.when(index + 1 < count)
    def _():
        for copy in halos:
            copy.start()

    loads[1].wait()
    spread(v_in, v_rows, PAD, limit)
    for load in loads[2:6]:
        load.wait()
    for i in range(3):
        spread_small(taps_in.at[i], taps, i * reach)
    spread_small(rate_in, grown, 0)
    spread_small(residue_in, scale, 0)
    scale[...] = scale[...] * jnp.sqrt(2.0 * grown[...])
    decay[...] = jnp.exp(-grown[...])

    def drive(first, states):
        keyed = short_block(k_rows, taps, reach, reach, first)
        valued = short_block(v_rows, taps, 2 * reach, reach, first)
        driven = [x * y for x, y in zip(keyed, valued)]
        for i in range(UNROLL):
            driven_rows[first + i] = driven[i]
        after = []
        for n in range(modes):
            d, state = decay[n], states[n]
            for i in range(UNROLL):
                state = driven[i] if state is None else d * state + driven[i]
            after.append(state)
        return tuple(after)

    zeros = (jnp.zeros((groups, LANES), F32),) * modes
    states = lax.fori_loop(1, blocks, lambda b, c: drive(b * UNROLL, c), zeros)
    for n in range(modes):
        ends[0, n] = states[n]

    pl.when(index >= 1)(lambda: [copy.wait_recv() for copy in halos] and None)

    @pl.when(index == 0)
    def _():
        halo[...] = jnp.zeros_like(halo)

    for i, dst in enumerate((q_rows, k_rows, v_rows)):
        row = lax.broadcasted_iota(jnp.int32, (PAD, LANES), 0) - PAD
        for group in range(groups):
            piece = halo[i, :, group * LANES : (group + 1) * LANES].astype(F32)[HALO - PAD :]
            dst[0:PAD, group, :] = jnp.where(row < limit, piece, 0.0)
    states = drive(0, (None,) * modes)
    for n in range(modes):
        ends[0, n] = ends[0, n] + jnp.exp(-float(rows - UNROLL) * grown[n]) * states[n]

    slot = 0
    rounds = []
    for stage, group in enumerate(shifts):
        copies = []
        for step in group:
            copies.append((step, slot, remote(
                ends.at[stage], incoming.at[slot], state_send.at[slot], state_recv.at[slot],
                index + step, place,
            )))
            slot += 1
        rounds.append(copies)

    def send(stage):
        for step, _, copy in rounds[stage]:
            pl.when(index + step < count)(copy.start)

    send(0)
    loads[6].wait()
    spread(q_in, q_rows, PAD, limit)
    gain = gain_in[...]

    def scan(gate, block, states):
        first = block * UNROLL
        driven = [driven_rows[first + i] for i in range(UNROLL)]
        total = [gain * x for x in driven]
        after = []
        for n in range(modes):
            state, d, a = states[n], decay[n], scale[n]
            for i in range(UNROLL):
                state = d * state + driven[i]
                total[i] = total[i] + a * state
            after.append(state)
        query = short_block(q_rows, taps, 0, reach, first)
        for i in range(UNROLL):
            if gate:
                mixed[first + i] = query[i] * total[i]
            else:
                partial_rows[first + i] = total[i]
                query_rows[first + i] = query[i]
        return tuple(after)

    cut = early * span // UNROLL
    states = zeros
    done = 0
    for stage, copies in enumerate(rounds):
        stop = cut * (stage + 1) // len(rounds)
        states = lax.fori_loop(done, stop, functools.partial(scan, False), states)
        done = stop
        first_round = stage == 0
        if first_round:
            ends[1] = jnp.zeros((modes, groups, LANES), F32)
        else:
            ends[stage + 1] = ends[stage]
        covered = 0 if first_round else copies[0][0]
        for step, where, copy in copies:
            factor = float((step - 1 if first_round else covered) * rows)

            @pl.when(index >= step)
            def _():
                copy.wait_recv()
                ends[stage + 1] = ends[stage + 1] + jnp.exp(-factor * grown[...]) * incoming[where]

        if stage + 1 < len(rounds):
            send(stage + 1)

    last = len(rounds)
    if cut < blocks:
        states = tuple(
            states[n] + jnp.exp(-float(cut * UNROLL) * grown[n]) * ends[last, n]
            for n in range(modes)
        )

    def correct(block, states):
        first = block * UNROLL
        total = [partial_rows[first + i] for i in range(UNROLL)]
        after = []
        for n in range(modes):
            state, d = states[n], decay[n]
            for i in range(UNROLL):
                total[i] = total[i] + state
                state = state * d
            after.append(state)
        for i in range(UNROLL):
            mixed[first + i] = total[i] * query_rows[first + i]
        return tuple(after)

    def gather(block, carry):
        first = pl.multiple_of(block * 64, 64)
        for group in range(groups):
            gated[pl.ds(first, 64), group * LANES : (group + 1) * LANES] = mixed[
                pl.ds(first, 64), group, :
            ]
        return carry

    loads[7].wait()
    loads[8].wait()
    order = list(range(early, spans)) + list(range(early))
    sends = {}
    per = span // UNROLL
    for s in order:
        if s == 0:
            states = tuple(scale[n] * decay[n] * ends[last, n] for n in range(modes))
        body = functools.partial(scan, True) if s >= early else correct
        states = lax.fori_loop(s * per, (s + 1) * per, body, states)
        lax.fori_loop(s * span // 64, (s + 1) * span // 64, gather, 0)
        tenant = tenant_ref[s]
        maps[0:rank, :] = proj_in[tenant].astype(F32)
        maps[rank : 2 * rank, :] = weight_in[tenant].astype(F32)
        both = maps[...].astype(BF16)
        value = gated[s * span : (s + 1) * span, :]
        high = value.astype(BF16)
        low = (value - high.astype(F32)).astype(BF16)
        dims = (((1,), (1,)), ((), ()))
        sums[s] = lax.dot_general(
            both, high, dims, preferred_element_type=F32
        ) + lax.dot_general(both, low, dims, preferred_element_type=F32)
        sends[s] = [
            remote(
                sums.at[s], arrived.at[offset - 1, s], sum_send.at[offset - 1, s],
                sum_recv.at[offset - 1, s], index, lax.rem(place + offset, places),
            )
            for offset in range(1, places)
        ]
        for copy in sends[s]:
            copy.start()

    line = lax.broadcasted_iota(jnp.int32, (2 * rank, span), 0)
    stores = []
    for s in order:
        tenant = tenant_ref[s]
        maps[0:rank, :] = proj_in[tenant].astype(F32)
        maps[rank : 2 * rank, :] = proj_in[tenant].astype(F32)
        totals = sums[s]
        for offset in range(1, places):
            sends[s][offset - 1].wait_recv()
            totals = totals + arrived[offset - 1, s]
        bias = jnp.zeros((2 * rank, span), F32)
        for r in range(rank):
            bias = jnp.where(line % rank == r, bias_ref[r, tenant], bias)
        change = pltpu.roll(totals, rank, 0) - totals
        delta = jnp.where(line < rank, change, -change) + bias
        high = delta.astype(BF16).astype(F32)
        parts = jnp.where(line < rank, high, delta - high).astype(BF16)
        edit = lax.dot_general(
            parts, maps[...].astype(BF16), (((0,), (0,)), ((), ())), preferred_element_type=F32
        )
        row = s * span + lax.broadcasted_iota(jnp.int32, (span, width), 0)
        value = gated[s * span : (s + 1) * span, :] + edit
        out_ref[s * span : (s + 1) * span, :] = jnp.where(row < limit, value, 0.0).astype(BF16)
        part = pl.ds(s * span, span)
        stores.append(pltpu.make_async_copy(out_ref.at[part], out_hbm.at[part], out_sem.at[s]))
        stores[-1].start()

    @pl.when(index + 1 < count)
    def _():
        for copy in halos:
            copy.wait_send()

    for copies in rounds:
        for step, _, copy in copies:
            pl.when(index + step < count)(copy.wait_send)
    for s in order:
        for copy in sends[s]:
            copy.wait_send()
    for store in stores:
        store.wait()


VMEM = pl.BlockSpec(memory_space=pltpu.VMEM)
SMEM = pl.BlockSpec(memory_space=pltpu.SMEM)
HBM = pl.BlockSpec(memory_space=pltpu.HBM)


def local(
    q_in, k_in, v_in, conv_weight, mode_residue, decay_rate, skip_gain, tenant_ids, valid_length,
    reft_proj, reft_weight, reft_bias,
):
    rows, width = q_in.shape
    groups = width // LANES
    modes = decay_rate.shape[0]
    reach = conv_weight.shape[1]
    rank = reft_bias.shape[1]
    spans = tenant_ids.shape[0]
    count, places = lax.axis_size("seq"), lax.axis_size("ch")
    shifts = [(1, 2)]
    while 2 ** len(shifts) < count:
        shifts.append((2 ** len(shifts),))
    slots = len(shifts) + 1
    gain = skip_gain.reshape(groups, LANES)
    args = (q_in, k_in, v_in, conv_weight, mode_residue, decay_rate, gain, reft_proj, reft_weight)
    tall = pltpu.VMEM((rows + PAD, groups, LANES), F32)
    cube = pltpu.VMEM((rows, groups, LANES), F32)
    small = pltpu.VMEM((modes, groups, LANES), F32)
    dma = pltpu.SemaphoreType.DMA
    return pl.pallas_call(
        functools.partial(kernel, spans - 1, tuple(shifts)),
        out_shape=jax.ShapeDtypeStruct((rows, width), BF16),
        in_specs=[SMEM] * 3 + [HBM] * 9,
        out_specs=HBM,
        scratch_shapes=[pltpu.VMEM(x.shape, x.dtype) for x in args]
        + [tall, tall, tall, cube, cube, cube, cube, pltpu.VMEM((rows, width), F32)]
        + [pltpu.VMEM((3 * reach, groups, LANES), F32), small, small, small]
        + [
            pltpu.VMEM((3, HALO, width), BF16),
            pltpu.VMEM((slots, modes, groups, LANES), F32),
            pltpu.VMEM((slots, modes, groups, LANES), F32),
            pltpu.VMEM((2 * rank, width), F32),
            pltpu.VMEM((spans, 2 * rank, rows // spans), F32),
            pltpu.VMEM((places - 1, spans, 2 * rank, rows // spans), F32),
        ]
        + [dma((len(args),)), dma((3,)), dma((3,)), dma((slots,)), dma((slots,))]
        + [dma((places - 1, spans)), dma((places - 1, spans))]
        + [pltpu.VMEM((rows, width), BF16), dma((spans,))],
        compiler_params=pltpu.CompilerParams(
            collective_id=0, has_side_effects=True, vmem_limit_bytes=60 * 2**20
        ),
    )(tenant_ids, valid_length, reft_bias.T, *args)


def solution(mesh):
    return jax.shard_map(
        local,
        mesh=mesh,
        in_specs=(
            P("seq", "ch"),
            P("seq", "ch"),
            P("seq", "ch"),
            P(None, None, "ch"),
            P(None, "ch"),
            P(None, "ch"),
            P("ch"),
            P("seq"),
            P(),
            P(None, None, "ch"),
            P(None, None, "ch"),
            P(),
        ),
        out_specs=P("seq", "ch"),
        check_vma=False,
    )
```
